256 devices in a mesh: chi: 64 (over x, z, core), site: 4 (over y).
Axes of the slice: x: 4, y: 4, z: 8, core: 2. Of those that a mesh axis runs over, the one named last changes fastest.
Arguments:
- upper: bfloat16 [4, 256, 256, 2401], P('site', 'chi'), may hold values from -6 to 6
- corner_low: bfloat16 [4, 256, 256], P('site'), may hold values from -0.375 to 0.375
- edge_bottom: bfloat16 [4, 256, 256, 49], P('site', None, 'chi'), may hold values from -6 to 6
- corner_right: bfloat16 [4, 256, 256], P('site'), may hold values from -0.375 to 0.375
- edge_right: bfloat16 [4, 256, 256, 49], P('site', 'chi'), may hold values from -6 to 6
- right_side: float32 [4, 2, 2401], P('site'), may hold values from -6 to 6
Outputs:
- solution_field: float32 [4, 2, 2401], P('site')
- residual: float32 [4, 2, 2401], P('site')
The draws below stay inside these ranges and needn't reach their ends.
All inputs are finite; a program needn't handle non-finite values.
Results may differ from the reference program's by a relative error of at most 0.033.
Values may be sent and summed in bfloat16 or wider, within the bound.
No kernel may reach another device: no remote copies, remote signals or barrier semaphores. Data moves between devices by JAX's collectives and lax.ppermute only.
A program may use at most 128 MiB of HBM per device.

```python
import math
import jax
import jax.numpy as jnp
from jax import lax

CHI = 256
D = 7
PHYS = 2
ITERS = 2
DD = 49
SITES = 4
N_CHI = 64


def block_scale(rng, extent, cuts, least, high):
    def one(dim, blocks):
        draws = jax.random.uniform(jax.random.fold_in(jax.random.fold_in(rng, 6), dim), (blocks,), jnp.float32, least / len(cuts), high / len(cuts))
        return jnp.repeat(jnp.exp(draws), extent[dim] // blocks).reshape((-1,) + (1,) * (len(extent) - dim - 1))

    loudness = one(*cuts[0])
    for cut in cuts[1:]:
        loudness = loudness * one(*cut)
    return loudness


def noise(key, shape, deviation, limit, split=(), kind=jnp.bfloat16):
    entries = jax.random.normal(key, shape, jnp.float32) * deviation
    if len(split) > 0:
        entries = block_scale(key, shape, split, -0.22, 0.18) * entries
    return jnp.clip(entries, min=-limit, max=limit).astype(kind)


def setup_inputs(seed: int = 0) -> dict:
    key_list = jax.random.split(jax.random.key(seed), 7)
    upper = noise(key_list[0], (SITES, CHI, CHI, DD * DD), 1.0, 6.0, ((0, 4), (1, 64)))
    corner_low = noise(key_list[1], (SITES, CHI, CHI), CHI ** -0.5, 0.375, ((0, 4),))
    edge_bottom = noise(key_list[2], (SITES, CHI, CHI, DD), 1.0, 6.0, ((0, 4), (2, 64)))
    corner_right = noise(key_list[3], (SITES, CHI, CHI), CHI ** -0.5, 0.375, ((0, 4),))
    edge_right = noise(key_list[4], (SITES, CHI, CHI, DD), 1.0, 6.0, ((0, 4), (1, 64)))
    right_side = noise(key_list[5], (SITES, PHYS, DD * DD), 1.0, 6.0, ((0, 4),), jnp.float32)
    return {"upper": upper, "corner_low": corner_low, "edge_bottom": edge_bottom, "corner_right": corner_right, "edge_right": edge_right, "right_side": right_side}


shift_value = 0.5

def lower_site(parts):
    corner_l, edge_b, corner_r, edge_r = parts
    mixed = jnp.dot(corner_l, edge_b.reshape(CHI, CHI * DD), preferred_element_type=jnp.float32).astype(jnp.bfloat16)
    columns = jnp.einsum('gf,efr->ger', corner_r.astype(jnp.float32), edge_r.astype(jnp.float32)).astype(jnp.bfloat16)
    quad_right = columns.astype(jnp.float32).reshape(CHI, CHI, D, D)
    blocks = mixed.astype(jnp.float32).reshape(N_CHI, CHI // N_CHI, CHI, D, D)

    def one_block(block):
        value = jnp.einsum('igab,gecd->ieacbd', block, quad_right) * (1.0 / math.sqrt(CHI))
        return value.astype(jnp.bfloat16)
    stacked = lax.map(one_block, blocks)
    return stacked.reshape(CHI, CHI, DD, DD)

def forward_site(parts):
    upper_site, lower_part, vector = parts
    quant = lax.optimization_barrier(vector.astype(jnp.bfloat16)).astype(jnp.float32)
    upper_blocks = upper_site.reshape(N_CHI, CHI // N_CHI, CHI, DD, DD)
    lower_blocks = lower_part.reshape(N_CHI, CHI // N_CHI, CHI, DD, DD)

    def advance(total, pair):
        sectioned = jnp.einsum('ieku,pkc->ieupc', pair[0].astype(jnp.float32), quant).astype(jnp.bfloat16)
        sectioned = lax.optimization_barrier(sectioned).astype(jnp.float32)
        return (total + jnp.einsum('ieupc,iecd->pud', sectioned, pair[1].astype(jnp.float32)), None)
    total, _ = lax.scan(advance, jnp.zeros((PHYS, DD, DD), jnp.float32), (upper_blocks, lower_blocks))
    return total * (1.0 / (CHI * DD))

def backward_site(parts):
    upper_site, lower_part, image = parts
    quant = lax.optimization_barrier(image.astype(jnp.bfloat16)).astype(jnp.float32)
    upper_blocks = upper_site.reshape(N_CHI, CHI // N_CHI, CHI, DD, DD)
    lower_blocks = lower_part.reshape(N_CHI, CHI // N_CHI, CHI, DD, DD)

    def advance(total, pair):
        sectioned = jnp.einsum('ieku,pud->iekpd', pair[0].astype(jnp.float32), quant).astype(jnp.bfloat16)
        sectioned = lax.optimization_barrier(sectioned).astype(jnp.float32)
        return (total + jnp.einsum('iekpd,iecd->pkc', sectioned, pair[1].astype(jnp.float32)), None)
    total, _ = lax.scan(advance, jnp.zeros((PHYS, DD, DD), jnp.float32), (upper_blocks, lower_blocks))
    return total * (1.0 / (CHI * DD))

def reference(upper, corner_low, edge_bottom, corner_right, edge_right, right_side):
    lower = lax.map(lower_site, (corner_low, edge_bottom, corner_right, edge_right))

    def metric(vector):
        image = lax.map(forward_site, (upper, lower, vector))
        back = lax.map(backward_site, (upper, lower, image))
        return back + shift_value * vector
    residual = right_side.reshape(SITES, PHYS, DD, DD)
    direction = residual
    solution = jnp.zeros_like(residual)
    norm_now = jnp.sum(residual * residual)
    for step in range(ITERS):
        image = metric(direction)
        alpha = norm_now / jnp.sum(direction * image)
        solution = solution + alpha * direction
        residual = residual - alpha * image
        norm_next = jnp.sum(residual * residual)
        direction = residual + norm_next / norm_now * direction
        norm_now = norm_next
    return (solution.reshape(SITES, PHYS, DD * DD), residual.reshape(SITES, PHYS, DD * DD))
```

```python
import math

import jax
import jax.numpy as jnp
from jax import lax
from jax.sharding import Mesh, PartitionSpec as P

CHI = 256
D = 7
PHYS = 2
ITERS = 2
DD = 49
BF = jnp.bfloat16
F32 = jnp.float32

shift_value = 0.5
scale_metric = 1.0 / (CHI * DD)


def spread(value, axes, count):
    return lax.all_to_all(jnp.broadcast_to(value[None], (count,) + value.shape), axes, 0, 0, tiled=True)


def swap(value):
    return lax.ppermute(value, "core", [(0, 1), (1, 0)])


def sum_chi(partial):
    core = lax.axis_index("core")
    flat = partial.reshape(PHYS, DD * DD)
    keep = jnp.where(core == 0, flat[0], flat[1])
    send = jnp.where(core == 0, flat[1], flat[0])
    keep = (keep + swap(send)).astype(BF)
    keep = jnp.pad(keep, (0, 19 * 128 - DD * DD)).reshape(19, 128)
    half = jnp.sum(spread(keep, ("x", "z"), 32).astype(F32), axis=0)
    other = swap(half)
    both = jnp.where(core == 0, jnp.stack([half, other]), jnp.stack([other, half]))
    return both.reshape(PHYS, 19 * 128)[:, : DD * DD].reshape(PHYS, DD, DD)


def sum_site(value):
    rows = jnp.broadcast_to(value, (8, 128))
    for step in (1, 2):
        rows = rows + lax.ppermute(rows, "site", [(i, i ^ step) for i in range(4)])
    return rows[0, 0]


def body(upper, corner_low, edge_bottom, corner_right, edge_right, right_side):
    local_rows = upper.shape[1]
    upper_five = upper[0].reshape(local_rows, CHI, DD, DD)
    part_mixed = jnp.dot(
        corner_low[0], edge_bottom[0].reshape(CHI, -1), preferred_element_type=F32
    )
    part_mixed = part_mixed.astype(BF).reshape(CHI, -1, DD)
    rows_lower = lax.all_to_all(part_mixed, ("x", "z", "core"), split_axis=0, concat_axis=1, tiled=True)
    quad_lower = rows_lower.reshape(local_rows, CHI, D, D)
    part_columns = jnp.einsum("gf,efr->ger", corner_right[0], edge_right[0], preferred_element_type=F32)
    part_columns = part_columns.astype(BF)
    stage = spread(part_columns.reshape(CHI * 4 * DD // 128, 128), "x", 4)
    stage = lax.all_gather(stage, "z")
    stage = lax.all_gather(stage, "core")
    segment = stage.reshape(2, 8, 4, CHI, 4, DD).transpose(3, 2, 1, 0, 4, 5)
    quad_right = segment.reshape(CHI, CHI, D, D)
    value = jnp.einsum("igab,gecd->ieacbd", quad_lower, quad_right, preferred_element_type=F32)
    value = value * (1.0 / math.sqrt(CHI))
    lower = value.reshape(local_rows, CHI, DD, DD).astype(BF)

    residual = right_side[0].reshape(PHYS, DD, DD)
    solution = jnp.zeros_like(residual)
    direction = residual
    norm_now = sum_site(jnp.sum(residual * residual))
    for step in range(ITERS):
        sectioned = jnp.einsum("ieku,pkc->ieupc", upper_five, direction.astype(BF), preferred_element_type=F32)
        partial = jnp.einsum("ieupc,iecd->pud", sectioned.astype(BF), lower, preferred_element_type=F32)
        quant = sum_chi(partial * scale_metric).astype(BF)
        sectioned = jnp.einsum("ieku,pud->iekpd", upper_five, quant, preferred_element_type=F32)
        partial = jnp.einsum("iekpd,iecd->pkc", sectioned.astype(BF), lower, preferred_element_type=F32)
        image = sum_chi(partial * scale_metric) + shift_value * direction
        alpha = norm_now / sum_site(jnp.sum(direction * image))
        solution = solution + alpha * direction
        residual = residual - alpha * image
        norm_next = sum_site(jnp.sum(residual * residual))
        direction = residual + norm_next / norm_now * direction
        norm_now = norm_next
    return (solution.reshape(1, PHYS, DD * DD), residual.reshape(1, PHYS, DD * DD))


def solution(mesh):
    split = Mesh(mesh.devices.reshape(4, 8, 2, 4), ("x", "z", "core", "site"))
    chi = ("x", "z", "core")
    placed = (
        P("site", chi, None, None),
        P("site", None, None),
        P("site", None, chi, None),
        P("site", None, None),
        P("site", chi, None, None),
        P("site", None, None),
    )
    return jax.shard_map(
        body,
        mesh=split,
        in_specs=placed,
        out_specs=(P("site", None, None), P("site", None, None)),
        check_vma=False,
    )
```

```python
import functools
import math

import jax
import jax.numpy as jnp
import numpy as np
from jax import lax
from jax.experimental import pallas as pl
from jax.experimental.pallas import tpu as pltpu
from jax.sharding import Mesh, PartitionSpec as P

CHI = 256
D = 7
PHYS = 2
DD = 49
BF = jnp.bfloat16
F32 = jnp.float32

NX, NZ, NCORE, NSITE = 4, 8, 2, 4
CHIPS = NX * NZ
ROWS_I = 8
COLS_E = 128
GROUP = 8
PAIR = D * GROUP
SLAB = 400
WIDE = 2432
BLOCKS = WIDE // 128
CHUNK = 80
STRIPE = 256
VEC = PHYS * PAIR

shift_value = 0.5
scale_metric = 1.0 / (CHI * DD)


def tables():
    lane = np.arange(WIDE)
    valid = lane < DD * DD
    first = np.zeros((128, WIDE), np.float32)
    first[(lane // DD)[valid], lane[valid]] = 1
    second = np.zeros((128, WIDE), np.float32)
    second[(lane % DD)[valid], lane[valid]] = 1
    fold = np.zeros((VEC, D * VEC), np.float32)
    for r in range(D):
        for p in range(PHYS):
            for q in range(D):
                for s in range(GROUP):
                    fold[p * PAIR + r * GROUP + q, r * VEC + p * PAIR + q * GROUP + s] = 1
    return first, second, fold


def parity_table():
    table = np.zeros((NCORE, COLS_E, CHI), np.float32)
    for c in range(NCORE):
        for z in range(NZ):
            for x in range(NX):
                for q in range(4):
                    table[c, (z * NX + x) * 4 + q, ((x * NZ + z) * NCORE + c) * 4 + q] = 1
    return table


def unpack(parts):
    low = lax.broadcasted_iota(jnp.int32, (32, 128), 1) < 64
    rows = []
    for half in parts:
        rows.append(jnp.where(low, half, 0.0))
        rows.append(jnp.where(low, pltpu.roll(half, 64, 1), 0.0)[:24])
    return jnp.concatenate(rows, axis=0)


def pack(rows):
    out = []
    for p in range(PHYS):
        upper_rows = jnp.concatenate([rows[p * PAIR + 32 : p * PAIR + 56], jnp.zeros((8, 128), F32)], axis=0)
        out.append(rows[p * PAIR : p * PAIR + 32] + pltpu.roll(upper_rows, 64, 1))
    return out


def two_terms(value):
    high = value.astype(BF)
    return high, (value - high.astype(F32)).astype(BF)


def dot(a, b):
    return jnp.dot(a, b, preferred_element_type=F32)


def dot_lanes(a, b):
    return lax.dot_general(a, b, (((1,), (1,)), ((), ())), preferred_element_type=F32)


def metric_kernel(mixed_ref, cols_ref, own_ref, other_ref, out_ref, low_ref):
    step = pl.program_id(0)

    @pl.when(step == 0)
    def _():
        for rk in range(D):
            cols = [cols_ref[:, rk * D + rb].reshape(COLS_E, CHI) for rb in range(D)]
            low = dot_lanes(mixed_ref[...], jnp.concatenate(cols, axis=0)) * (1.0 / math.sqrt(CHI))
            for i in range(ROWS_I):
                strip = [low[i * PAIR : (i + 1) * PAIR, rb * COLS_E : (rb + 1) * COLS_E] for rb in range(D)]
                strip.append(jnp.zeros((SLAB - D * PAIR, COLS_E), F32))
                strip = jnp.concatenate(strip, axis=0).astype(BF)
                low_ref[rk, :, i * COLS_E : (i + 1) * COLS_E] = strip

    half = range(ROWS_I // 2)
    upper = jnp.concatenate([own_ref[i] for i in half] + [other_ref[i] for i in half], axis=1)
    inside = lax.broadcasted_iota(jnp.int32, (1, STRIPE), 1) + step * STRIPE < DD * DD
    for rk in range(D):
        out_ref[rk] = jnp.where(inside, dot_lanes(low_ref[rk], upper), 0.0).astype(BF)


def build_metric(mixed, cols, own, other):
    stripe = pl.BlockSpec((ROWS_I // 2, STRIPE, COLS_E), lambda n: (0, n, 0))
    return pl.pallas_call(
        metric_kernel,
        grid=(pl.cdiv(WIDE, STRIPE),),
        in_specs=[
            pl.BlockSpec((ROWS_I * PAIR, CHI), lambda n: (0, 0)),
            pl.BlockSpec((NZ, DD, 16, CHI), lambda n: (0, 0, 0, 0)),
            stripe,
            stripe,
        ],
        out_specs=pl.BlockSpec((D, SLAB, STRIPE), lambda n: (0, 0, n)),
        out_shape=pltpu.HBM((D, SLAB, WIDE), BF),
        scratch_shapes=[pltpu.VMEM((D, SLAB, ROWS_I * COLS_E), BF)],
        compiler_params=pltpu.CompilerParams(vmem_limit_bytes=30 * 1024 * 1024),
        cost_estimate=pl.CostEstimate(flops=15_000_000_000, bytes_accessed=22_000_000, transcendentals=0),
        name="build_metric",
    )(mixed, *(pltpu.with_memory_space_constraint(a, pltpu.HBM) for a in (cols, own, other)))


def forward_step(step, metric_ref, e_ref, acc_ref):
    for block in range(BLOCKS):
        lanes = slice(block * 128, (block + 1) * 128)
        tile = metric_ref[step, :, lanes].astype(F32)
        for p in range(PHYS):
            eight = e_ref[pl.ds(pl.multiple_of(p * PAIR + step * GROUP, GROUP), GROUP), lanes]
            factors = [jnp.broadcast_to(eight[q : q + 1], (GROUP, 128)) for q in range(D)]
            for rb in range(D):
                total = acc_ref[p * PAIR + rb * GROUP : p * PAIR + (rb + 1) * GROUP, lanes]
                for q in range(D):
                    row = (rb * D + q) * GROUP
                    total = total + tile[row : row + GROUP] * factors[q]
                acc_ref[p * PAIR + rb * GROUP : p * PAIR + (rb + 1) * GROUP, lanes] = total


def backward_step(step, metric_ref, f_ref, z_ref):
    for block in range(BLOCKS):
        lanes = slice(block * 128, (block + 1) * 128)
        tile = metric_ref[step, :, lanes].astype(F32)
        for p in range(PHYS):
            factors = [f_ref[p * PAIR + rb * GROUP : p * PAIR + (rb + 1) * GROUP, lanes] for rb in range(D)]
            for q in range(D):
                total = tile[q * GROUP : (q + 1) * GROUP] * factors[0]
                for rb in range(1, D):
                    row = (rb * D + q) * GROUP
                    total = total + tile[row : row + GROUP] * factors[rb]
                z_ref[step, p * PAIR + q * GROUP : p * PAIR + (q + 1) * GROUP, lanes] = total


def halves(core_ref, own_ref, other_ref):
    first = core_ref[0] == 0
    own, other = own_ref[...], other_ref[...]
    return [jnp.where(first, own, other), jnp.where(first, other, own)]


def lane_sums(parts):
    total = parts[0]
    for part in parts[1:]:
        total = total + part
    return jnp.sum(total, axis=0, keepdims=True)


def whole(row_ref):
    return jnp.sum(row_ref[...], axis=1, keepdims=True)


def apply_kernel(forward, prologue, n_in, n_out, core_ref, *refs):
    metric_ref, expand_ref, reduce_ref, fold_ref = refs[:4]
    ins, outs = refs[4 : 4 + n_in], refs[4 + n_in : 4 + n_in + n_out]
    keep_ref, send_ref, wide_ref, sum_ref, slab_ref, sems = refs[4 + n_in + n_out :]
    step = pl.program_id(0)

    def fetch(r, c):
        rows = pl.ds(c * CHUNK, CHUNK)
        return pltpu.make_async_copy(metric_ref.at[r, rows], slab_ref.at[r, rows], sems.at[r, c])

    @pl.when(step == 0)
    def _():
        for r in range(D):
            for c in range(SLAB // CHUNK):
                fetch(r, c).start()
        vec = prologue(core_ref, ins, outs)
        wide_ref[...] = dot(unpack(vec).astype(BF), expand_ref[...])
        if forward:
            sum_ref[...] = jnp.zeros_like(sum_ref)

    for c in range(SLAB // CHUNK):
        fetch(step, c).wait()
    (forward_step if forward else backward_step)(step, slab_ref, wide_ref, sum_ref)

    @pl.when(step == D - 1)
    def _():
        if forward:
            high, low = two_terms(sum_ref[...])
            rows = dot(high, reduce_ref[...]) + dot(low, reduce_ref[...])
        else:
            sums = [dot(sum_ref[r].astype(BF), reduce_ref[...]) for r in range(D)]
            high, low = two_terms(jnp.concatenate(sums, axis=0))
            rows = dot(fold_ref[...], high) + dot(fold_ref[...], low)
        parts = pack(rows * scale_metric)
        first = core_ref[0] == 0
        keep_ref[...] = jnp.where(first, parts[0], parts[1])
        send_ref[...] = jnp.where(first, parts[1], parts[0])


def full(shape):
    return pl.BlockSpec(shape, lambda *r: (0,) * len(shape))


VECTOR = jax.ShapeDtypeStruct((PHYS, 32, 128), F32)
HALF = jax.ShapeDtypeStruct((32, 128), F32)
LANES = jax.ShapeDtypeStruct((1, 128), F32)


def apply_metric(forward, prologue, core, metric, constants, ins, outs):
    wide = pltpu.VMEM((VEC, WIDE), F32)
    out_shape = list(outs) + [HALF, HALF]
    return pl.pallas_call(
        functools.partial(apply_kernel, forward, prologue, len(ins), len(outs)),
        grid=(D,),
        in_specs=[pl.BlockSpec(memory_space=pltpu.SMEM), pl.BlockSpec(memory_space=pl.ANY)]
        + [full(c.shape) for c in constants]
        + [full(i.shape) for i in ins],
        out_specs=[full(o.shape) for o in out_shape],
        out_shape=out_shape,
        scratch_shapes=[
            wide,
            wide if forward else pltpu.VMEM((D, VEC, WIDE), F32),
            pltpu.VMEM((D, SLAB, WIDE), BF),
            pltpu.SemaphoreType.DMA((D, SLAB // CHUNK)),
        ],
        compiler_params=pltpu.CompilerParams(vmem_limit_bytes=34 * 1024 * 1024),
        cost_estimate=pl.CostEstimate(flops=50_000_000, bytes_accessed=14_000_000, transcendentals=0),
        name="forward" if forward else "backward",
    )(core, pltpu.with_memory_space_constraint(metric, pltpu.HBM), *constants, *ins)


def first_vector(core_ref, ins, outs):
    return [ins[0][p] for p in range(PHYS)]


def first_image(core_ref, ins, outs):
    own_ref, other_ref, start_ref = ins
    image_ref, curve_ref = outs
    image = halves(core_ref, own_ref, other_ref)
    parts = []
    for p in range(PHYS):
        image_ref[p] = image[p]
        parts.append(image[p] * image[p] + shift_value * (start_ref[p] * start_ref[p]))
    curve_ref[...] = lane_sums(parts)
    return image


def next_residual(core_ref, ins, outs):
    own_ref, other_ref, start_ref, norm_ref, curve_ref = ins
    residual_ref, next_ref = outs
    back = halves(core_ref, own_ref, other_ref)
    alpha = whole(norm_ref) / whole(curve_ref)
    residual = [start_ref[p] - alpha * (back[p] + shift_value * start_ref[p]) for p in range(PHYS)]
    for p in range(PHYS):
        residual_ref[p] = residual[p]
    next_ref[...] = lane_sums([r * r for r in residual])
    return residual


def next_image(core_ref, ins, outs):
    own_ref, other_ref, start_ref, image_ref, residual_ref, norm_ref, next_ref = ins
    direction_ref, curve_ref = outs
    image = halves(core_ref, own_ref, other_ref)
    beta = whole(next_ref) / whole(norm_ref)
    image = [image[p] + beta * image_ref[p] for p in range(PHYS)]
    parts = []
    for p in range(PHYS):
        direction = residual_ref[p] + beta * start_ref[p]
        direction_ref[p] = direction
        parts.append(image[p] * image[p] + shift_value * (direction * direction))
    curve_ref[...] = lane_sums(parts)
    return image


def finish_kernel(core_ref, own_ref, other_ref, start_ref, residual_ref, direction_ref, norm_ref, curve_ref, next_ref,
                  last_ref, solution_ref, out_ref):
    back = halves(core_ref, own_ref, other_ref)
    alpha_0 = whole(norm_ref) / whole(curve_ref)
    alpha_1 = whole(next_ref) / whole(last_ref)
    for p in range(PHYS):
        direction = direction_ref[p]
        solution_ref[p] = alpha_0 * start_ref[p] + alpha_1 * direction
        out_ref[p] = residual_ref[p] - alpha_1 * (back[p] + shift_value * direction)


def finish(core, *ins):
    return pl.pallas_call(
        finish_kernel,
        in_specs=[pl.BlockSpec(memory_space=pltpu.SMEM)] + [full(i.shape) for i in ins],
        out_specs=[full(VECTOR.shape)] * 2,
        out_shape=[VECTOR, VECTOR],
        name="finish",
    )(core, *ins)


def spread(value, axes, count):
    return lax.all_to_all(jnp.broadcast_to(value[None], (count,) + value.shape), axes, 0, 0, tiled=True)


def swap(value):
    return lax.ppermute(value, "core", [(0, 1), (1, 0)])


def sum_chi(keep, send, lanes=None):
    keep = (keep + swap(send)).astype(BF)
    parts = spread(keep, ("x", "z"), CHIPS)
    if lanes is not None:
        for step in (1, 2):
            lanes = lanes + lax.ppermute(lanes, "site", [(i, i ^ step) for i in range(NSITE)])
        parts, lanes = lax.optimization_barrier((parts, lanes))
    half = jnp.sum(parts.astype(F32), axis=0)
    pair = (half, swap(half))
    return pair if lanes is None else (pair, lanes)


def to_packed(field):
    move = np.zeros((2, 32, DD), np.float32)
    for dk in range(D):
        for rk in range(D):
            move[rk // 4, rk % 4 * GROUP + dk, dk * D + rk] = 1
    grid = jnp.einsum("hrc,pkc->prhk", move, field.reshape(PHYS, DD, DD), precision=lax.Precision.HIGHEST)
    return jnp.pad(grid, ((0, 0), (0, 0), (0, 0), (0, 64 - DD))).reshape(PHYS, 32, 128)


def from_packed(packed):
    grid = packed.reshape(PHYS, 4, 8, 2, 64).transpose(0, 4, 3, 1, 2).reshape(PHYS, 64, 8, 8)
    return grid[:, :DD, :D, :D].transpose(0, 1, 3, 2).reshape(1, PHYS, DD * DD)


def body(upper, corner_low, edge_bottom, corner_right, edge_right, right_side):
    core = lax.axis_index("core")

    cols = jnp.einsum("efr,gf->reg", edge_right[0], corner_right[0], preferred_element_type=F32).astype(BF)
    cols = spread(cols.reshape(DD * 4 * CHI // 128, 128), "x", NX)
    cols = cols.reshape(NX, DD, 4, CHI).transpose(1, 0, 2, 3).reshape(DD, 4 * NX, CHI)
    cols_all = lax.all_gather(cols, "z")

    mixed = jnp.einsum("ih,hgq->giq", corner_low[0], edge_bottom[0], preferred_element_type=F32).astype(BF)
    mixed = mixed.reshape(4, 64, 4, DD).transpose(1, 0, 2, 3)
    mixed = lax.all_to_all(mixed, ("x", "z", "core"), 0, 0, tiled=True).reshape(CHI, 4, DD)
    rows = np.zeros((PAIR, DD), np.float32)
    rows[np.arange(DD) // D * GROUP + np.arange(DD) % D, np.arange(DD)] = 1
    mixed = jnp.einsum("rq,giq->irg", jnp.asarray(rows, BF), mixed, preferred_element_type=F32).astype(BF)
    mixed = mixed.reshape(4 * PAIR, CHI)
    mixed = jnp.concatenate([mixed, swap(mixed)], axis=0)

    pick = jnp.asarray(parity_table(), BF)
    choose = lambda c: jnp.einsum(
        "je,iek->ikj", lax.dynamic_index_in_dim(pick, c, 0, keepdims=False), upper[0], preferred_element_type=F32
    ).astype(BF)
    other = swap(choose(1 - core))
    own = choose(core)

    metric = build_metric(mixed, cols_all, own, other)

    first, second, fold = (jnp.asarray(t, BF) for t in tables())
    flag = core.astype(jnp.int32).reshape(1)
    forward = functools.partial(apply_metric, True)
    backward = functools.partial(apply_metric, False)
    ahead, behind = (first, second.T, fold), (second, first.T, fold)

    start = to_packed(right_side[0])
    keep, send = forward(first_vector, flag, metric, ahead, [start], [])
    pair, norm_0 = sum_chi(keep, send, jnp.sum(start * start, axis=(0, 1))[None])
    image, curve_0, keep, send = backward(first_image, flag, metric, behind, [*pair, start], [VECTOR, LANES])
    pair, curve_0 = sum_chi(keep, send, curve_0)
    residual, norm_1, keep, send = forward(
        next_residual, flag, metric, ahead, [*pair, start, norm_0, curve_0], [VECTOR, LANES]
    )
    pair, norm_1 = sum_chi(keep, send, norm_1)
    direction, curve_1, keep, send = backward(
        next_image, flag, metric, behind, [*pair, start, image, residual, norm_0, norm_1], [VECTOR, LANES]
    )
    pair, curve_1 = sum_chi(keep, send, curve_1)
    answer, residual = finish(flag, *pair, start, residual, direction, norm_0, curve_0, norm_1, curve_1)
    return from_packed(answer), from_packed(residual)


def solution(mesh):
    split = Mesh(mesh.devices.reshape(NX, NZ, NCORE, NSITE), ("x", "z", "core", "site"))
    chi = ("x", "z", "core")
    placed = (
        P("site", chi, None, None),
        P("site", None, None),
        P("site", None, chi, None),
        P("site", None, None),
        P("site", chi, None, None),
        P("site", None, None),
    )
    return jax.shard_map(
        body,
        mesh=split,
        in_specs=placed,
        out_specs=(P("site", None, None), P("site", None, None)),
        check_vma=False,
    )
```

```python
import functools
import math

import jax
import jax.numpy as jnp
import numpy as np
from jax import lax
from jax.experimental import pallas as pl
from jax.experimental.pallas import tpu as pltpu
from jax.sharding import Mesh, PartitionSpec as P

CHI = 256
D = 7
PHYS = 2
DD = 49
BF = jnp.bfloat16
F32 = jnp.float32

NX, NZ, NCORE, NSITE = 4, 8, 2, 4
CHIPS = NX * NZ
ROWS_I = 8
GROUP = 8
PAIR = D * GROUP
RB = 4
SLAB = RB * PAIR
WIDE = 2432
BLOCKS = WIDE // 128
CHUNK = 112
STRIPE = 512
PART = 128
OFFSETS = (0, -1, 1, -2, 2, -3, 3, 4)
VEC = PHYS * PAIR
IMG = PHYS * RB * GROUP

shift_value = 0.5
scale_metric = 1.0 / (CHI * DD)


def tables():
    lane = np.arange(WIDE)
    valid = lane < DD * DD
    first = np.zeros((128, WIDE), np.float32)
    first[(lane // DD)[valid], lane[valid]] = 1
    second = np.zeros((128, WIDE), np.float32)
    second[(lane % DD)[valid], lane[valid]] = 1
    fold = np.zeros((VEC, D * VEC), np.float32)
    for r in range(D):
        for p in range(PHYS):
            for q in range(D):
                for s in range(GROUP):
                    fold[p * PAIR + r * GROUP + q, r * VEC + p * PAIR + q * GROUP + s] = 1
    own = np.zeros((PAIR, WIDE), np.float32)
    for r in range(D):
        for q in range(D):
            own[r * GROUP + q] = second[q * D + r]
    return first, second, fold, own


def low_lanes():
    return lax.broadcasted_iota(jnp.int32, (32, 128), 1) < 64


def unpack(parts):
    rows = []
    for half in parts:
        rows.append(jnp.where(low_lanes(), half, 0.0))
        rows.append(jnp.where(low_lanes(), pltpu.roll(half, 64, 1), 0.0)[:24])
    return jnp.concatenate(rows, axis=0)


def pack(rows):
    out = []
    for p in range(PHYS):
        upper_rows = jnp.concatenate([rows[p * PAIR + 32 : p * PAIR + 56], jnp.zeros((8, 128), F32)], axis=0)
        out.append(rows[p * PAIR : p * PAIR + 32] + pltpu.roll(upper_rows, 64, 1))
    return out


def unpack_image(both):
    return jnp.concatenate(
        [jnp.where(low_lanes(), both, 0.0), jnp.where(low_lanes(), pltpu.roll(both, 64, 1), 0.0)], axis=0
    )


def pack_image(rows):
    return rows[:32] + pltpu.roll(rows[32:], 64, 1)


def two_terms(value):
    high = value.astype(BF)
    return high, (value - high.astype(F32)).astype(BF)


def dot(a, b):
    return jnp.dot(a, b, preferred_element_type=F32)


def dot_lanes(a, b):
    return lax.dot_general(a, b, (((1,), (1,)), ((), ())), preferred_element_type=F32)


def metric_kernel(n_blocks, more, mixed_ref, *refs):
    blocks, refs = refs[:n_blocks], refs[n_blocks:]
    own_ref, other_ref = refs[:2]
    out_ref, low_ref = refs[-2:]

    def block(b, pair):
        if b < 3 or n_blocks == 4:
            return blocks[b][pair]
        here = pair // (D * RB // 2)
        return blocks[3 + here][pair - here * (D * RB // 2)]

    @pl.when(pl.program_id(0) == 0)
    def _():
        for rk in range(D):
            cols = [block(b, rk * RB + rb) for rb in range(RB) for b in range(4)]
            low = dot_lanes(mixed_ref[...], jnp.concatenate(cols, axis=0)) * (1.0 / math.sqrt(CHI))
            for i in range(ROWS_I):
                strip = [low[i * PAIR : (i + 1) * PAIR, rb * PART : (rb + 1) * PART] for rb in range(RB)]
                low_ref[rk * SLAB : (rk + 1) * SLAB, i * PART : (i + 1) * PART] = jnp.concatenate(strip, axis=0).astype(BF)

    half = range(ROWS_I // 2)
    upper = jnp.concatenate([own_ref[i] for i in half] + [other_ref[i] for i in half], axis=1)
    value = dot_lanes(low_ref[...], upper)
    for rk in range(D):
        slab = value[rk * SLAB : (rk + 1) * SLAB]
        if more:
            slab = slab + refs[2][rk].astype(F32)
        out_ref[rk] = slab.astype(BF)


def build_metric(mixed, blocks, own, other, before=None):
    part = 0 if before is None else 1
    stripe = pl.BlockSpec((ROWS_I // 2, STRIPE, PART), lambda n: (0, n, part))
    result = pl.BlockSpec((D, SLAB, STRIPE), lambda n: (0, 0, n))
    arrays = [*blocks, own, other] + ([] if before is None else [before])
    return pl.pallas_call(
        functools.partial(metric_kernel, len(blocks), before is not None),
        grid=(pl.cdiv(WIDE, STRIPE),),
        in_specs=[full(mixed.shape)] + [full(b.shape) for b in blocks] + [stripe, stripe]
        + ([] if before is None else [result]),
        out_specs=result,
        out_shape=pltpu.HBM((D, SLAB, WIDE), BF),
        scratch_shapes=[pltpu.VMEM((D * SLAB, ROWS_I * PART), BF)],
        compiler_params=pltpu.CompilerParams(vmem_limit_bytes=34 * 1024 * 1024),
        cost_estimate=pl.CostEstimate(flops=8_000_000_000, bytes_accessed=22_000_000, transcendentals=0),
        name="build_first" if before is None else "build_second",
    )(mixed, *(pltpu.with_memory_space_constraint(a, pltpu.HBM) for a in arrays))


def full(shape):
    return pl.BlockSpec(shape, lambda *r: (0,) * len(shape))


def forward_step(step, metric_ref, e_ref, acc_ref):
    for block in range(BLOCKS):
        lanes = slice(block * 128, (block + 1) * 128)
        tile = metric_ref[step, :, lanes].astype(F32)
        for p in range(PHYS):
            eight = e_ref[pl.ds(pl.multiple_of(p * PAIR + step * GROUP, GROUP), GROUP), lanes]
            factors = [jnp.broadcast_to(eight[q : q + 1], (GROUP, 128)) for q in range(D)]
            for rb in range(RB):
                place = slice((p * RB + rb) * GROUP, (p * RB + rb + 1) * GROUP)
                total = acc_ref[place, lanes]
                for q in range(D):
                    row = (rb * D + q) * GROUP
                    total = total + tile[row : row + GROUP] * factors[q]
                acc_ref[place, lanes] = total


def backward_step(step, metric_ref, f_ref, z_ref):
    for block in range(BLOCKS):
        lanes = slice(block * 128, (block + 1) * 128)
        tile = metric_ref[step, :, lanes].astype(F32)
        for p in range(PHYS):
            factors = [f_ref[(p * RB + rb) * GROUP : (p * RB + rb + 1) * GROUP, lanes] for rb in range(RB)]
            for q in range(D):
                total = tile[q * GROUP : (q + 1) * GROUP] * factors[0]
                for rb in range(1, RB):
                    row = (rb * D + q) * GROUP
                    total = total + tile[row : row + GROUP] * factors[rb]
                z_ref[step, p * PAIR + q * GROUP : p * PAIR + (q + 1) * GROUP, lanes] = total


def halves(core_ref, own_ref, other_ref):
    first = core_ref[0] == 0
    own, other = own_ref[...], other_ref[...]
    return [jnp.where(first, own, other), jnp.where(first, other, own)]


def lane_sums(parts):
    total = parts[0]
    for part in parts[1:]:
        total = total + part
    return jnp.sum(total, axis=0, keepdims=True)


def apply_kernel(forward, prologue, n_in, n_out, core_ref, *refs):
    metric_ref, expand_ref, reduce_ref, fold_ref = refs[:4]
    ins, outs = refs[4 : 4 + n_in], refs[4 + n_in : 4 + n_in + n_out]
    wide_ref, sum_ref, slab_ref, sems = refs[-4:]
    step = pl.program_id(0)

    def fetch(r, c):
        rows = pl.ds(c * CHUNK, CHUNK)
        return pltpu.make_async_copy(metric_ref.at[r, rows], slab_ref.at[r, rows], sems.at[r, c])

    @pl.when(step == 0)
    def _():
        for r in range(D):
            for c in range(SLAB // CHUNK):
                fetch(r, c).start()
        vec = prologue(core_ref, ins, outs)
        rows = unpack(vec) if forward else unpack_image(vec)
        wide_ref[...] = dot(rows.astype(BF), expand_ref[...])
        if forward:
            sum_ref[...] = jnp.zeros_like(sum_ref)

    for c in range(SLAB // CHUNK):
        fetch(step, c).wait()
    (forward_step if forward else backward_step)(step, slab_ref, wide_ref, sum_ref)

    @pl.when(step == D - 1)
    def _():
        if forward:
            high, low = two_terms(sum_ref[...])
            rows = dot(high, reduce_ref[...]) + dot(low, reduce_ref[...])
            refs[-5][...] = pack_image(rows * scale_metric)
        else:
            sums = [dot(sum_ref[r].astype(BF), reduce_ref[...]) for r in range(D)]
            high, low = two_terms(jnp.concatenate(sums, axis=0))
            rows = dot(fold_ref[...], high) + dot(fold_ref[...], low)
            parts = pack(rows * scale_metric)
            first = core_ref[0] == 0
            refs[-6][...] = jnp.where(first, parts[0], parts[1])
            refs[-5][...] = jnp.where(first, parts[1], parts[0])


VECTOR = jax.ShapeDtypeStruct((PHYS, 32, 128), F32)
HALF = jax.ShapeDtypeStruct((32, 128), F32)


def sum_rows(count):
    return jax.ShapeDtypeStruct((count, 128), F32)


def apply_metric(forward, prologue, core, metric, constants, ins, outs):
    out_shape = list(outs) + ([HALF] if forward else [HALF, HALF])
    return pl.pallas_call(
        functools.partial(apply_kernel, forward, prologue, len(ins), len(outs)),
        grid=(D,),
        in_specs=[pl.BlockSpec(memory_space=pltpu.SMEM), pl.BlockSpec(memory_space=pl.ANY)]
        + [full(c.shape) for c in constants]
        + [full(i.shape) for i in ins],
        out_specs=[full(o.shape) for o in out_shape],
        out_shape=out_shape,
        scratch_shapes=[
            pltpu.VMEM((VEC if forward else IMG, WIDE), F32),
            pltpu.VMEM((IMG, WIDE) if forward else (D, VEC, WIDE), F32),
            pltpu.VMEM((D, SLAB, WIDE), BF),
            pltpu.SemaphoreType.DMA((D, SLAB // CHUNK)),
        ],
        compiler_params=pltpu.CompilerParams(vmem_limit_bytes=30 * 1024 * 1024),
        cost_estimate=pl.CostEstimate(flops=50_000_000, bytes_accessed=8_000_000, transcendentals=0),
        name="forward" if forward else "backward",
    )(core, pltpu.with_memory_space_constraint(metric, pltpu.HBM), *constants, *ins)


def first_vector(core_ref, ins, outs):
    return [ins[0][p] for p in range(PHYS)]


def share(a, b):
    return (shift_value / NCORE) * (a * b)


def sums_of(*groups):
    return jnp.concatenate([lane_sums(group) for group in groups], axis=0)


def first_image(core_ref, ins, outs):
    image = ins[0][...]
    start = [ins[1][p] for p in range(PHYS)]
    outs[0][...] = sums_of([image * image] + [share(v, v) for v in start], [v * v / NCORE for v in start])
    return image


def row(sums_ref, n):
    return jnp.sum(sums_ref[n : n + 1], axis=1, keepdims=True)


def next_residual(core_ref, ins, outs):
    own_ref, other_ref, start_ref, sums_ref = ins
    back = halves(core_ref, own_ref, other_ref)
    alpha = row(sums_ref, 1) / row(sums_ref, 0)
    residual = [start_ref[p] - alpha * (back[p] + shift_value * start_ref[p]) for p in range(PHYS)]
    for p in range(PHYS):
        outs[0][p] = residual[p]
    return residual


def next_image(core_ref, ins, outs):
    image, first = ins[0][...], ins[1][...]
    residual = [ins[2][p] for p in range(PHYS)]
    start = [ins[3][p] for p in range(PHYS)]
    outs[0][...] = sums_of(
        [image * image] + [share(r, r) for r in residual],
        [image * first] + [share(r, d) for r, d in zip(residual, start)],
        [r * r / NCORE for r in residual],
    )
    return image


def flatten(parts, expand_ref, own_ref):
    rest = unpack(parts)
    wide = None
    for _ in range(3):
        term = rest.astype(BF)
        rest = rest - term.astype(F32)
        piece = dot(term, expand_ref[...])
        wide = piece if wide is None else wide + piece
    own = own_ref[...].astype(F32)
    rows = [jnp.sum(wide[p * PAIR : (p + 1) * PAIR] * own, axis=0, keepdims=True) for p in range(PHYS)]
    return jnp.concatenate(rows, axis=0)[:, : DD * DD]


def finish_kernel(core_ref, expand_ref, own_lane_ref, half_0_ref, other_0_ref, half_1_ref, other_1_ref,
                  start_ref, residual_ref, sums_0_ref, sums_1_ref, solution_ref, out_ref):
    back_0 = halves(core_ref, half_0_ref, other_0_ref)
    back_r = halves(core_ref, half_1_ref, other_1_ref)
    curve_0, norm_0 = row(sums_0_ref, 0), row(sums_0_ref, 1)
    norm_1 = row(sums_1_ref, 2)
    alpha_0 = norm_0 / curve_0
    beta = norm_1 / norm_0
    curve_1 = row(sums_1_ref, 0) + beta * (2.0 * row(sums_1_ref, 1) + beta * curve_0)
    alpha_1 = norm_1 / curve_1
    answer, residual = [], []
    for p in range(PHYS):
        direction = residual_ref[p] + beta * start_ref[p]
        back = back_r[p] + beta * back_0[p] + shift_value * direction
        answer.append(alpha_0 * start_ref[p] + alpha_1 * direction)
        residual.append(residual_ref[p] - alpha_1 * back)
    solution_ref[0] = flatten(answer, expand_ref, own_lane_ref)
    out_ref[0] = flatten(residual, expand_ref, own_lane_ref)


def finish(core, *ins):
    field = jax.ShapeDtypeStruct((1, PHYS, DD * DD), F32)
    return pl.pallas_call(
        finish_kernel,
        in_specs=[pl.BlockSpec(memory_space=pltpu.SMEM)] + [full(i.shape) for i in ins],
        out_specs=[full(field.shape)] * 2,
        out_shape=[field, field],
        compiler_params=pltpu.CompilerParams(vmem_limit_bytes=16 * 1024 * 1024),
        name="finish",
    )(core, *ins)


def spread(value, axes, count):
    return lax.all_to_all(jnp.broadcast_to(value[None], (count,) + value.shape), axes, 0, 0, tiled=True)


def swap(value):
    return lax.ppermute(value, "core", [(0, 1), (1, 0)])


def sum_sites(lanes):
    for step in (1, 2):
        lanes = lanes + lax.ppermute(lanes, "site", [(i, i ^ step) for i in range(NSITE)])
    return lanes


def sum_chips(value, lanes=None, cores=False):
    parts = spread(value.astype(BF), ("x", "z"), CHIPS)
    if lanes is not None:
        lanes = sum_sites(lanes)
        if cores:
            lanes = lanes + swap(lanes)
        parts, lanes = lax.optimization_barrier((parts, lanes))
    return jnp.sum(parts.astype(F32), axis=0), lanes


def sum_halves(keep, send, lanes):
    half, lanes = sum_chips(keep + swap(send), lanes, True)
    return half, swap(half), lanes


def to_packed(field):
    move = np.zeros((2, 32, DD), np.float32)
    for dk in range(D):
        for rk in range(D):
            move[rk // 4, rk % 4 * GROUP + dk, dk * D + rk] = 1
    grid = jnp.einsum("hrc,pkc->prhk", move, field.reshape(PHYS, DD, DD), precision=lax.Precision.HIGHEST)
    return jnp.pad(grid, ((0, 0), (0, 0), (0, 0), (0, 64 - DD))).reshape(PHYS, 32, 128)


def ring(value, step):
    return lax.ppermute(value, "z", [(i, (i + step) % NZ) for i in range(NZ)])


def body(upper, corner_low, edge_bottom, corner_right, edge_right, right_side):
    core = lax.axis_index("core")

    mixed = jnp.einsum("ih,hgq->giq", corner_low[0], edge_bottom[0], preferred_element_type=F32).astype(BF)
    mixed = mixed.reshape(4, 64, 4, DD).transpose(1, 0, 2, 3)

    cols = jnp.einsum("efr,gf->reg", edge_right[0], corner_right[0], preferred_element_type=F32).astype(BF)
    cols = jnp.pad(cols.reshape(D, D, 4, CHI), ((0, 0), (0, 1), (0, 0), (0, 0))).reshape(D, NCORE, RB, 4, CHI)
    mine = lax.dynamic_index_in_dim(cols, core, 1, keepdims=False)
    other = swap(lax.dynamic_index_in_dim(cols, 1 - core, 1, keepdims=False))
    cols = jnp.stack([jnp.where(core == 0, mine, other), jnp.where(core == 0, other, mine)], axis=2)
    cols = spread(cols.reshape(D * RB * 8 * CHI // 128, 128), "x", NX)
    cols = cols.reshape(NX, D * RB, 8, CHI).transpose(1, 0, 2, 3).reshape(D * RB, 8 * NX, CHI)

    row = jnp.arange(CHI)
    z = (lax.axis_index("z") + jnp.asarray(OFFSETS)[row // 32] + NZ) % NZ
    place = (row // 8 % NX * NZ + z) * 8 + row % 8
    pick = (place[:, None] == jnp.arange(CHI)[None, :]).astype(BF)
    own = jnp.einsum("je,iek->ikj", pick, upper[0], preferred_element_type=F32).astype(BF)
    own = jnp.pad(own, ((0, 0), (0, WIDE - DD * DD), (0, 0)))

    cols, mixed, own = lax.optimization_barrier((cols, mixed, own))
    other = swap(own)
    up, down = [cols], [cols]
    for _ in range(2):
        up.append(ring(up[-1], 1))
        down.append(ring(down[-1], -1))

    rows = np.zeros((PAIR, DD), np.float32)
    rows[np.arange(DD) // D * GROUP + np.arange(DD) % D, np.arange(DD)] = 1
    mixed = lax.all_to_all(mixed, ("x", "z", "core"), 0, 0, tiled=True).reshape(CHI, 4, DD)
    mixed = jnp.einsum("rq,giq->irg", jnp.asarray(rows, BF), mixed, preferred_element_type=F32).astype(BF)
    mixed = mixed.reshape(4 * PAIR, CHI)
    mixed = jnp.concatenate([mixed, swap(mixed)], axis=0)
    start = to_packed(right_side[0])

    up.append(ring(up[-1], 1))
    down.append(ring(down[-1], -1))
    metric = build_metric(mixed, [cols, up[1], down[1], up[2]], own, other)
    far_up, far_down, metric = lax.optimization_barrier((up[3], down[3], metric))
    last = [ring(far_up[: D * RB // 2], 1), ring(far_down[D * RB // 2 :], -1)]
    metric = build_metric(mixed, [down[2], far_up, far_down, *last], own, other, metric)

    first, second, fold, own_lane = (jnp.asarray(t, BF) for t in tables())
    flag = core.astype(jnp.int32).reshape(1)
    forward = functools.partial(apply_metric, True)
    backward = functools.partial(apply_metric, False)
    ahead, behind = (first, second.T, fold), (second, first.T, fold)

    (part,) = forward(first_vector, flag, metric, ahead, [start], [])
    image, _ = sum_chips(part)
    sums_0, keep, send = backward(first_image, flag, metric, behind, [image, start], [sum_rows(2)])
    half_0, other_0, sums_0 = sum_halves(keep, send, sums_0)
    residual, part = forward(next_residual, flag, metric, ahead, [half_0, other_0, start, sums_0], [VECTOR])
    image_r, _ = sum_chips(part)
    sums_1, keep, send = backward(next_image, flag, metric, behind, [image_r, image, residual, start], [sum_rows(3)])
    half_1, other_1, sums_1 = sum_halves(keep, send, sums_1)
    return finish(flag, first, own_lane, half_0, other_0, half_1, other_1, start, residual, sums_0, sums_1)


def solution(mesh):
    split = Mesh(mesh.devices.reshape(NX, NZ, NCORE, NSITE), ("x", "z", "core", "site"))
    chi = ("x", "z", "core")
    placed = (
        P("site", chi, None, None),
        P("site", None, None),
        P("site", None, chi, None),
        P("site", None, None),
        P("site", chi, None, None),
        P("site", None, None),
    )
    return jax.shard_map(
        body,
        mesh=split,
        in_specs=placed,
        out_specs=(P("site", None, None), P("site", None, None)),
        check_vma=False,
    )
```

```python
import functools
import math

import jax
import jax.numpy as jnp
import numpy as np
from jax import lax
from jax.experimental import pallas as pl
from jax.experimental.pallas import tpu as pltpu
from jax.sharding import Mesh, PartitionSpec as P

CHI = 256
D = 7
PHYS = 2
DD = 49
BF = jnp.bfloat16
F32 = jnp.float32

NX, NZ, NCORE, NSITE = 4, 8, 2, 4
CHIPS = NX * NZ
ROWS_I = 8
GROUP = 8
PAIR = D * GROUP
RB = 4
SLAB = RB * PAIR
WIDE = 2432
BLOCKS = WIDE // 128
CHUNK = 112
STRIPE = 512
PART = 128
OFFSETS = (0, -1, 1, -2, 2, -3, 3, 4)
VEC = PHYS * PAIR
IMG = PHYS * RB * GROUP

shift_value = 0.5
scale_metric = 1.0 / (CHI * DD)


def tables():
    lane = np.arange(WIDE)
    valid = lane < DD * DD
    first = np.zeros((128, WIDE), np.float32)
    first[(lane // DD)[valid], lane[valid]] = 1
    second = np.zeros((128, WIDE), np.float32)
    second[(lane % DD)[valid], lane[valid]] = 1
    fold = np.zeros((VEC, D * VEC), np.float32)
    for r in range(D):
        for p in range(PHYS):
            for q in range(D):
                for s in range(GROUP):
                    fold[p * PAIR + r * GROUP + q, r * VEC + p * PAIR + q * GROUP + s] = 1
    own = np.zeros((PAIR, WIDE), np.float32)
    for r in range(D):
        for q in range(D):
            own[r * GROUP + q] = second[q * D + r]
    return first, second, fold, own


def low_lanes():
    return lax.broadcasted_iota(jnp.int32, (32, 128), 1) < 64


def unpack(parts):
    rows = []
    for half in parts:
        rows.append(jnp.where(low_lanes(), half, 0.0))
        rows.append(jnp.where(low_lanes(), pltpu.roll(half, 64, 1), 0.0)[:24])
    return jnp.concatenate(rows, axis=0)


def pack(rows):
    out = []
    for p in range(PHYS):
        upper_rows = jnp.concatenate([rows[p * PAIR + 32 : p * PAIR + 56], jnp.zeros((8, 128), F32)], axis=0)
        out.append(rows[p * PAIR : p * PAIR + 32] + pltpu.roll(upper_rows, 64, 1))
    return out


def unpack_image(both):
    return jnp.concatenate(
        [jnp.where(low_lanes(), both, 0.0), jnp.where(low_lanes(), pltpu.roll(both, 64, 1), 0.0)], axis=0
    )


def pack_image(rows):
    return rows[:32] + pltpu.roll(rows[32:], 64, 1)


def two_terms(value):
    high = value.astype(BF)
    return high, (value - high.astype(F32)).astype(BF)


def dot(a, b):
    return jnp.dot(a, b, preferred_element_type=F32)


def dot_lanes(a, b):
    return lax.dot_general(a, b, (((1,), (1,)), ((), ())), preferred_element_type=F32)


def metric_kernel(n_blocks, more, mixed_ref, *refs):
    blocks, refs = refs[:n_blocks], refs[n_blocks:]
    own_ref, other_ref = refs[:2]
    out_ref, low_ref = refs[-2:]

    def block(b, pair):
        if b < 3 or n_blocks == 4:
            return blocks[b][pair]
        here = pair // (D * RB // 2)
        return blocks[3 + here][pair - here * (D * RB // 2)]

    @pl.when(pl.program_id(0) == 0)
    def _():
        for rk in range(D):
            cols = [block(b, rk * RB + rb) for rb in range(RB) for b in range(4)]
            low = dot_lanes(mixed_ref[...], jnp.concatenate(cols, axis=0)) * (1.0 / math.sqrt(CHI))
            for i in range(ROWS_I):
                strip = [low[i * PAIR : (i + 1) * PAIR, rb * PART : (rb + 1) * PART] for rb in range(RB)]
                low_ref[rk * SLAB : (rk + 1) * SLAB, i * PART : (i + 1) * PART] = jnp.concatenate(strip, axis=0).astype(BF)

    half = range(ROWS_I // 2)
    upper = jnp.concatenate([own_ref[i] for i in half] + [other_ref[i] for i in half], axis=1)
    value = dot_lanes(low_ref[...], upper)
    for rk in range(D):
        slab = value[rk * SLAB : (rk + 1) * SLAB]
        if more:
            slab = slab + refs[2][rk].astype(F32)
        out_ref[rk] = slab.astype(BF)


def build_metric(mixed, blocks, own, other, before=None):
    part = 0 if before is None else 1
    stripe = pl.BlockSpec((ROWS_I // 2, STRIPE, PART), lambda n: (0, n, part))
    result = pl.BlockSpec((D, SLAB, STRIPE), lambda n: (0, 0, n))
    arrays = [*blocks, own, other] + ([] if before is None else [before])
    return pl.pallas_call(
        functools.partial(metric_kernel, len(blocks), before is not None),
        grid=(pl.cdiv(WIDE, STRIPE),),
        in_specs=[full(mixed.shape)] + [full(b.shape) for b in blocks] + [stripe, stripe]
        + ([] if before is None else [result]),
        out_specs=result,
        out_shape=pltpu.HBM((D, SLAB, WIDE), BF),
        scratch_shapes=[pltpu.VMEM((D * SLAB, ROWS_I * PART), BF)],
        compiler_params=pltpu.CompilerParams(vmem_limit_bytes=34 * 1024 * 1024),
        cost_estimate=pl.CostEstimate(flops=8_000_000_000, bytes_accessed=22_000_000, transcendentals=0),
        name="build_first" if before is None else "build_second",
    )(mixed, *(pltpu.with_memory_space_constraint(a, pltpu.HBM) for a in arrays))


def full(shape):
    return pl.BlockSpec(shape, lambda *r: (0,) * len(shape))


def forward_step(step, metric_ref, e_ref, acc_ref):
    for block in range(BLOCKS):
        lanes = slice(block * 128, (block + 1) * 128)
        tile = metric_ref[step, :, lanes].astype(F32)
        for p in range(PHYS):
            eight = e_ref[pl.ds(pl.multiple_of(p * PAIR + step * GROUP, GROUP), GROUP), lanes]
            factors = [jnp.broadcast_to(eight[q : q + 1], (GROUP, 128)) for q in range(D)]
            for rb in range(RB):
                place = slice((p * RB + rb) * GROUP, (p * RB + rb + 1) * GROUP)
                total = acc_ref[place, lanes]
                for q in range(D):
                    row = (rb * D + q) * GROUP
                    total = total + tile[row : row + GROUP] * factors[q]
                acc_ref[place, lanes] = total


def backward_step(step, metric_ref, f_ref, z_ref):
    for block in range(BLOCKS):
        lanes = slice(block * 128, (block + 1) * 128)
        tile = metric_ref[step, :, lanes].astype(F32)
        for p in range(PHYS):
            factors = [f_ref[(p * RB + rb) * GROUP : (p * RB + rb + 1) * GROUP, lanes] for rb in range(RB)]
            for q in range(D):
                total = tile[q * GROUP : (q + 1) * GROUP] * factors[0]
                for rb in range(1, RB):
                    row = (rb * D + q) * GROUP
                    total = total + tile[row : row + GROUP] * factors[rb]
                z_ref[step, p * PAIR + q * GROUP : p * PAIR + (q + 1) * GROUP, lanes] = total


def halves(core_ref, own_ref, other_ref):
    first = core_ref[0] == 0
    own, other = own_ref[...], other_ref[...]
    return [jnp.where(first, own, other), jnp.where(first, other, own)]


def lane_sums(parts):
    total = parts[0]
    for part in parts[1:]:
        total = total + part
    return jnp.sum(total, axis=0, keepdims=True)


def apply_kernel(forward, prologue, n_in, n_out, core_ref, *refs):
    metric_ref, expand_ref, reduce_ref, fold_ref = refs[:4]
    ins, outs = refs[4 : 4 + n_in], refs[4 + n_in : 4 + n_in + n_out]
    wide_ref, sum_ref, slab_ref, sems = refs[-4:]
    step = pl.program_id(0)

    def fetch(r, c):
        rows = pl.ds(c * CHUNK, CHUNK)
        return pltpu.make_async_copy(metric_ref.at[r, rows], slab_ref.at[r, rows], sems.at[r, c])

    @pl.when(step == 0)
    def _():
        for r in range(D):
            for c in range(SLAB // CHUNK):
                fetch(r, c).start()
        vec = prologue(core_ref, ins, outs)
        rows = unpack(vec) if forward else unpack_image(vec)
        wide_ref[...] = dot(rows.astype(BF), expand_ref[...])
        if forward:
            sum_ref[...] = jnp.zeros_like(sum_ref)

    for c in range(SLAB // CHUNK):
        fetch(step, c).wait()
    (forward_step if forward else backward_step)(step, slab_ref, wide_ref, sum_ref)

    @pl.when(step == D - 1)
    def _():
        if forward:
            high, low = two_terms(sum_ref[...])
            rows = dot(high, reduce_ref[...]) + dot(low, reduce_ref[...])
            refs[-5][...] = pack_image(rows * scale_metric)
        else:
            sums = [dot(sum_ref[r].astype(BF), reduce_ref[...]) for r in range(D)]
            high, low = two_terms(jnp.concatenate(sums, axis=0))
            rows = dot(fold_ref[...], high) + dot(fold_ref[...], low)
            parts = pack(rows * scale_metric)
            first = core_ref[0] == 0
            refs[-6][...] = jnp.where(first, parts[0], parts[1])
            refs[-5][...] = jnp.where(first, parts[1], parts[0])


VECTOR = jax.ShapeDtypeStruct((PHYS, 32, 128), F32)
HALF = jax.ShapeDtypeStruct((32, 128), F32)


def sum_rows(count):
    return jax.ShapeDtypeStruct((count, 128), F32)


def apply_metric(forward, prologue, core, metric, constants, ins, outs):
    out_shape = list(outs) + ([HALF] if forward else [HALF, HALF])
    return pl.pallas_call(
        functools.partial(apply_kernel, forward, prologue, len(ins), len(outs)),
        grid=(D,),
        in_specs=[pl.BlockSpec(memory_space=pltpu.SMEM), pl.BlockSpec(memory_space=pl.ANY)]
        + [full(c.shape) for c in constants]
        + [full(i.shape) for i in ins],
        out_specs=[full(o.shape) for o in out_shape],
        out_shape=out_shape,
        scratch_shapes=[
            pltpu.VMEM((VEC if forward else IMG, WIDE), F32),
            pltpu.VMEM((IMG, WIDE) if forward else (D, VEC, WIDE), F32),
            pltpu.VMEM((D, SLAB, WIDE), BF),
            pltpu.SemaphoreType.DMA((D, SLAB // CHUNK)),
        ],
        compiler_params=pltpu.CompilerParams(vmem_limit_bytes=30 * 1024 * 1024),
        cost_estimate=pl.CostEstimate(flops=50_000_000, bytes_accessed=8_000_000, transcendentals=0),
        name="forward" if forward else "backward",
    )(core, pltpu.with_memory_space_constraint(metric, pltpu.HBM), *constants, *ins)


def first_vector(core_ref, ins, outs):
    return [ins[0][p] for p in range(PHYS)]


def share(a, b):
    return (shift_value / NCORE) * (a * b)


def sums_of(*groups):
    return jnp.concatenate([lane_sums(group) for group in groups], axis=0)


def first_image(core_ref, ins, outs):
    image = ins[0][...]
    start = [ins[1][p] for p in range(PHYS)]
    outs[0][...] = sums_of([image * image] + [share(v, v) for v in start], [v * v / NCORE for v in start])
    return image


def row(sums_ref, n):
    return jnp.sum(sums_ref[n : n + 1], axis=1, keepdims=True)


def next_residual(core_ref, ins, outs):
    own_ref, other_ref, start_ref, sums_ref = ins
    back = halves(core_ref, own_ref, other_ref)
    alpha = row(sums_ref, 1) / row(sums_ref, 0)
    residual = [start_ref[p] - alpha * (back[p] + shift_value * start_ref[p]) for p in range(PHYS)]
    for p in range(PHYS):
        outs[0][p] = residual[p]
    return residual


def next_image(core_ref, ins, outs):
    image, first = ins[0][...], ins[1][...]
    residual = [ins[2][p] for p in range(PHYS)]
    start = [ins[3][p] for p in range(PHYS)]
    outs[0][...] = sums_of(
        [image * image] + [share(r, r) for r in residual],
        [image * first] + [share(r, d) for r, d in zip(residual, start)],
        [r * r / NCORE for r in residual],
    )
    return image


def flatten(parts, expand_ref, own_ref):
    rest = unpack(parts)
    wide = None
    for _ in range(3):
        term = rest.astype(BF)
        rest = rest - term.astype(F32)
        piece = dot(term, expand_ref[...])
        wide = piece if wide is None else wide + piece
    own = own_ref[...].astype(F32)
    rows = [jnp.sum(wide[p * PAIR : (p + 1) * PAIR] * own, axis=0, keepdims=True) for p in range(PHYS)]
    return jnp.concatenate(rows, axis=0)[:, : DD * DD]


def finish_kernel(core_ref, expand_ref, own_lane_ref, half_0_ref, other_0_ref, half_1_ref, other_1_ref,
                  start_ref, residual_ref, sums_0_ref, sums_1_ref, solution_ref, out_ref):
    back_0 = halves(core_ref, half_0_ref, other_0_ref)
    back_r = halves(core_ref, half_1_ref, other_1_ref)
    curve_0, norm_0 = row(sums_0_ref, 0), row(sums_0_ref, 1)
    norm_1 = row(sums_1_ref, 2)
    alpha_0 = norm_0 / curve_0
    beta = norm_1 / norm_0
    curve_1 = row(sums_1_ref, 0) + beta * (2.0 * row(sums_1_ref, 1) + beta * curve_0)
    alpha_1 = norm_1 / curve_1
    answer, residual = [], []
    for p in range(PHYS):
        direction = residual_ref[p] + beta * start_ref[p]
        back = back_r[p] + beta * back_0[p] + shift_value * direction
        answer.append(alpha_0 * start_ref[p] + alpha_1 * direction)
        residual.append(residual_ref[p] - alpha_1 * back)
    solution_ref[0] = flatten(answer, expand_ref, own_lane_ref)
    out_ref[0] = flatten(residual, expand_ref, own_lane_ref)


def finish(core, *ins):
    field = jax.ShapeDtypeStruct((1, PHYS, DD * DD), F32)
    return pl.pallas_call(
        finish_kernel,
        in_specs=[pl.BlockSpec(memory_space=pltpu.SMEM)] + [full(i.shape) for i in ins],
        out_specs=[full(field.shape)] * 2,
        out_shape=[field, field],
        compiler_params=pltpu.CompilerParams(vmem_limit_bytes=16 * 1024 * 1024),
        name="finish",
    )(core, *ins)


def spread(value, axes, count):
    return lax.all_to_all(jnp.broadcast_to(value[None], (count,) + value.shape), axes, 0, 0, tiled=True)


def swap(value):
    return lax.ppermute(value, "core", [(0, 1), (1, 0)])


def sum_sites(lanes):
    others = [lax.ppermute(lanes, "site", [(i, i ^ step) for i in range(NSITE)]) for step in (1, 2, 3)]
    return lanes + others[0] + others[1] + others[2]


def sum_chips(value, lanes=None, cores=False):
    parts = spread(value.astype(BF), ("x", "z"), CHIPS)
    if lanes is not None:
        if cores:
            lanes = lanes + swap(lanes)
        lanes = sum_sites(lanes)
        parts, lanes = lax.optimization_barrier((parts, lanes))
    return jnp.sum(parts.astype(F32), axis=0), lanes


def sum_halves(keep, send, lanes):
    half, lanes = sum_chips(keep + swap(send), lanes, True)
    return half, swap(half), lanes


def to_packed(field):
    move = np.zeros((2, 32, DD), np.float32)
    for dk in range(D):
        for rk in range(D):
            move[rk // 4, rk % 4 * GROUP + dk, dk * D + rk] = 1
    grid = jnp.einsum("hrc,pkc->prhk", move, field.reshape(PHYS, DD, DD), precision=lax.Precision.HIGHEST)
    return jnp.pad(grid, ((0, 0), (0, 0), (0, 0), (0, 64 - DD))).reshape(PHYS, 32, 128)


def ring(value, step):
    return lax.ppermute(value, "z", [(i, (i + step) % NZ) for i in range(NZ)])


def body(upper, corner_low, edge_bottom, corner_right, edge_right, right_side):
    core = lax.axis_index("core")

    mixed = jnp.einsum("ih,hgq->giq", corner_low[0], edge_bottom[0], preferred_element_type=F32).astype(BF)
    mixed = mixed.reshape(4, 64, 4, DD).transpose(1, 0, 2, 3)

    cols = jnp.einsum("efr,gf->reg", edge_right[0], corner_right[0], preferred_element_type=F32).astype(BF)
    cols = jnp.pad(cols.reshape(D, D, 4, CHI), ((0, 0), (0, 1), (0, 0), (0, 0))).reshape(D, NCORE, RB, 4, CHI)
    mine = lax.dynamic_index_in_dim(cols, core, 1, keepdims=False)
    other = swap(lax.dynamic_index_in_dim(cols, 1 - core, 1, keepdims=False))
    cols = jnp.stack([jnp.where(core == 0, mine, other), jnp.where(core == 0, other, mine)], axis=2)
    cols = spread(cols.reshape(D * RB * 8 * CHI // 128, 128), "x", NX)
    cols = cols.reshape(NX, D * RB, 8, CHI).transpose(1, 0, 2, 3).reshape(D * RB, 8 * NX, CHI)

    row = jnp.arange(CHI)
    z = (lax.axis_index("z") + jnp.asarray(OFFSETS)[row // 32] + NZ) % NZ
    place = (row // 8 % NX * NZ + z) * 8 + row % 8
    pick = (place[:, None] == jnp.arange(CHI)[None, :]).astype(BF)
    own = jnp.einsum("je,iek->ikj", pick, upper[0], preferred_element_type=F32).astype(BF)
    own = jnp.pad(own, ((0, 0), (0, WIDE - DD * DD), (0, 0)))

    cols, mixed, own = lax.optimization_barrier((cols, mixed, own))
    other = swap(own)
    up, down = [cols], [cols]
    for _ in range(2):
        up.append(ring(up[-1], 1))
        down.append(ring(down[-1], -1))

    rows = np.zeros((PAIR, DD), np.float32)
    rows[np.arange(DD) // D * GROUP + np.arange(DD) % D, np.arange(DD)] = 1
    mixed = lax.all_to_all(mixed, ("x", "z", "core"), 0, 0, tiled=True).reshape(CHI, 4, DD)
    mixed = jnp.einsum("rq,giq->irg", jnp.asarray(rows, BF), mixed, preferred_element_type=F32).astype(BF)
    mixed = mixed.reshape(4 * PAIR, CHI)
    mixed = jnp.concatenate([mixed, swap(mixed)], axis=0)
    start = to_packed(right_side[0])

    up.append(ring(up[-1], 1))
    down.append(ring(down[-1], -1))
    metric = build_metric(mixed, [cols, up[1], down[1], up[2]], own, other)
    far_up, far_down, metric = lax.optimization_barrier((up[3], down[3], metric))
    last = [ring(far_up[: D * RB // 2], 1), ring(far_down[D * RB // 2 :], -1)]
    metric = build_metric(mixed, [down[2], far_up, far_down, *last], own, other, metric)

    first, second, fold, own_lane = (jnp.asarray(t, BF) for t in tables())
    flag = core.astype(jnp.int32).reshape(1)
    forward = functools.partial(apply_metric, True)
    backward = functools.partial(apply_metric, False)
    ahead, behind = (first, second.T, fold), (second, first.T, fold)

    (part,) = forward(first_vector, flag, metric, ahead, [start], [])
    image, _ = sum_chips(part)
    sums_0, keep, send = backward(first_image, flag, metric, behind, [image, start], [sum_rows(2)])
    half_0, other_0, sums_0 = sum_halves(keep, send, sums_0)
    residual, part = forward(next_residual, flag, metric, ahead, [half_0, other_0, start, sums_0], [VECTOR])
    image_r, _ = sum_chips(part)
    sums_1, keep, send = backward(next_image, flag, metric, behind, [image_r, image, residual, start], [sum_rows(3)])
    half_1, other_1, sums_1 = sum_halves(keep, send, sums_1)
    return finish(flag, first, own_lane, half_0, other_0, half_1, other_1, start, residual, sums_0, sums_1)


def solution(mesh):
    split = Mesh(mesh.devices.reshape(NX, NZ, NCORE, NSITE), ("x", "z", "core", "site"))
    chi = ("x", "z", "core")
    placed = (
        P("site", chi, None, None),
        P("site", None, None),
        P("site", None, chi, None),
        P("site", None, None),
        P("site", chi, None, None),
        P("site", None, None),
    )
    return jax.shard_map(
        body,
        mesh=split,
        in_specs=placed,
        out_specs=(P("site", None, None), P("site", None, None)),
        check_vma=False,
    )
```

```python
import functools
import math

import jax
import jax.numpy as jnp
import numpy as np
from jax import lax
from jax.experimental import pallas as pl
from jax.experimental.pallas import tpu as pltpu
from jax.sharding import Mesh, PartitionSpec as P

CHI = 256
D = 7
PHYS = 2
DD = 49
BF = jnp.bfloat16
F32 = jnp.float32

NX, NZ, NCORE, NSITE = 4, 8, 2, 4
CHIPS = NX * NZ
ROWS_I = 8
GROUP = 8
PAIR = D * GROUP
RB = 4
SLAB = RB * PAIR
WIDE = 2432
BLOCKS = WIDE // 128
CHUNK = 112
STRIPE = 512
PART = 128
OFFSETS = (0, -1, 1, -2, 2, -3, 3, 4)
VEC = PHYS * PAIR
IMG = PHYS * RB * GROUP

shift_value = 0.5
scale_metric = 1.0 / (CHI * DD)


def tables():
    lane = np.arange(WIDE)
    valid = lane < DD * DD
    first = np.zeros((128, WIDE), np.float32)
    first[(lane // DD)[valid], lane[valid]] = 1
    second = np.zeros((128, WIDE), np.float32)
    second[(lane % DD)[valid], lane[valid]] = 1
    fold = np.zeros((VEC, D * VEC), np.float32)
    for r in range(D):
        for p in range(PHYS):
            for q in range(D):
                for s in range(GROUP):
                    fold[p * PAIR + r * GROUP + q, r * VEC + p * PAIR + q * GROUP + s] = 1
    own = np.zeros((PAIR, WIDE), np.float32)
    for r in range(D):
        for q in range(D):
            own[r * GROUP + q] = second[q * D + r]
    return first, second, fold, own


def low_lanes():
    return lax.broadcasted_iota(jnp.int32, (32, 128), 1) < 64


def unpack(parts):
    rows = []
    for half in parts:
        rows.append(jnp.where(low_lanes(), half, 0.0))
        rows.append(jnp.where(low_lanes(), pltpu.roll(half, 64, 1), 0.0)[:24])
    return jnp.concatenate(rows, axis=0)


def pack(rows):
    out = []
    for p in range(PHYS):
        upper_rows = jnp.concatenate([rows[p * PAIR + 32 : p * PAIR + 56], jnp.zeros((8, 128), F32)], axis=0)
        out.append(rows[p * PAIR : p * PAIR + 32] + pltpu.roll(upper_rows, 64, 1))
    return out


def unpack_image(both):
    return jnp.concatenate(
        [jnp.where(low_lanes(), both, 0.0), jnp.where(low_lanes(), pltpu.roll(both, 64, 1), 0.0)], axis=0
    )


def pack_image(rows):
    return rows[:32] + pltpu.roll(rows[32:], 64, 1)


def two_terms(value):
    high = value.astype(BF)
    return high, (value - high.astype(F32)).astype(BF)


def dot(a, b):
    return jnp.dot(a, b, preferred_element_type=F32)


def dot_lanes(a, b):
    return lax.dot_general(a, b, (((1,), (1,)), ((), ())), preferred_element_type=F32)


def metric_kernel(n_blocks, more, mixed_ref, *refs):
    blocks, refs = refs[:n_blocks], refs[n_blocks:]
    own_ref, other_ref = refs[:2]
    out_ref, low_ref = refs[-2:]

    def block(b, pair):
        if b < 3 or n_blocks == 4:
            return blocks[b][pair]
        here = pair // (D * RB // 2)
        return blocks[3 + here][pair - here * (D * RB // 2)]

    @pl.when(pl.program_id(0) == 0)
    def _():
        for rk in range(D):
            cols = [block(b, rk * RB + rb) for rb in range(RB) for b in range(4)]
            low = dot_lanes(mixed_ref[...], jnp.concatenate(cols, axis=0)) * (1.0 / math.sqrt(CHI))
            for i in range(ROWS_I):
                strip = [low[i * PAIR : (i + 1) * PAIR, rb * PART : (rb + 1) * PART] for rb in range(RB)]
                low_ref[rk * SLAB : (rk + 1) * SLAB, i * PART : (i + 1) * PART] = jnp.concatenate(strip, axis=0).astype(BF)

    half = range(ROWS_I // 2)
    upper = jnp.concatenate([own_ref[i] for i in half] + [other_ref[i] for i in half], axis=1)
    value = dot_lanes(low_ref[...], upper)
    for rk in range(D):
        slab = value[rk * SLAB : (rk + 1) * SLAB]
        if more:
            slab = slab + refs[2][rk].astype(F32)
        out_ref[rk] = slab.astype(BF)


def build_metric(mixed, blocks, own, other, before=None):
    part = 0 if before is None else 1
    stripe = pl.BlockSpec((ROWS_I // 2, STRIPE, PART), lambda n: (0, n, part))
    result = pl.BlockSpec((D, SLAB, STRIPE), lambda n: (0, 0, n))
    arrays = [*blocks, own, other] + ([] if before is None else [before])
    return pl.pallas_call(
        functools.partial(metric_kernel, len(blocks), before is not None),
        grid=(pl.cdiv(WIDE, STRIPE),),
        in_specs=[full(mixed.shape)] + [full(b.shape) for b in blocks] + [stripe, stripe]
        + ([] if before is None else [result]),
        out_specs=result,
        out_shape=pltpu.HBM((D, SLAB, WIDE), BF),
        scratch_shapes=[pltpu.VMEM((D * SLAB, ROWS_I * PART), BF)],
        compiler_params=pltpu.CompilerParams(vmem_limit_bytes=34 * 1024 * 1024),
        cost_estimate=pl.CostEstimate(flops=8_000_000_000, bytes_accessed=22_000_000, transcendentals=0),
        name="build_first" if before is None else "build_second",
    )(mixed, *(pltpu.with_memory_space_constraint(a, pltpu.HBM) for a in arrays))


def full(shape):
    return pl.BlockSpec(shape, lambda *r: (0,) * len(shape))


def forward_step(step, metric_ref, e_ref, acc_ref):
    for block in range(BLOCKS):
        lanes = slice(block * 128, (block + 1) * 128)
        tile = metric_ref[step, :, lanes].astype(F32)
        for p in range(PHYS):
            eight = e_ref[pl.ds(pl.multiple_of(p * PAIR + step * GROUP, GROUP), GROUP), lanes]
            factors = [jnp.broadcast_to(eight[q : q + 1], (GROUP, 128)) for q in range(D)]
            for rb in range(RB):
                place = slice((p * RB + rb) * GROUP, (p * RB + rb + 1) * GROUP)
                total = acc_ref[place, lanes]
                for q in range(D):
                    row = (rb * D + q) * GROUP
                    total = total + tile[row : row + GROUP] * factors[q]
                acc_ref[place, lanes] = total


def backward_step(step, metric_ref, f_ref, z_ref):
    for block in range(BLOCKS):
        lanes = slice(block * 128, (block + 1) * 128)
        tile = metric_ref[step, :, lanes].astype(F32)
        for p in range(PHYS):
            factors = [f_ref[(p * RB + rb) * GROUP : (p * RB + rb + 1) * GROUP, lanes] for rb in range(RB)]
            for q in range(D):
                total = tile[q * GROUP : (q + 1) * GROUP] * factors[0]
                for rb in range(1, RB):
                    row = (rb * D + q) * GROUP
                    total = total + tile[row : row + GROUP] * factors[rb]
                z_ref[step, p * PAIR + q * GROUP : p * PAIR + (q + 1) * GROUP, lanes] = total


def halves(core_ref, own_ref, other_ref):
    first = core_ref[0] == 0
    own, other = own_ref[...], other_ref[...]
    return [jnp.where(first, own, other), jnp.where(first, other, own)]


def lane_sums(parts):
    total = parts[0]
    for part in parts[1:]:
        total = total + part
    return jnp.sum(total, axis=0, keepdims=True)


def apply_kernel(forward, prologue, n_in, n_out, core_ref, *refs):
    metric_ref, expand_ref, reduce_ref, fold_ref = refs[:4]
    ins, outs = refs[4 : 4 + n_in], refs[4 + n_in : 4 + n_in + n_out]
    wide_ref, sum_ref, slab_ref, sems = refs[-4:]
    step = pl.program_id(0)

    def fetch(r, c):
        rows = pl.ds(c * CHUNK, CHUNK)
        return pltpu.make_async_copy(metric_ref.at[r, rows], slab_ref.at[r, rows], sems.at[r, c])

    @pl.when(step == 0)
    def _():
        for r in range(D):
            for c in range(SLAB // CHUNK):
                fetch(r, c).start()
        vec = prologue(core_ref, ins, outs)
        rows = unpack(vec) if forward else unpack_image(vec)
        wide_ref[...] = dot(rows.astype(BF), expand_ref[...])
        if forward:
            sum_ref[...] = jnp.zeros_like(sum_ref)

    for c in range(SLAB // CHUNK):
        fetch(step, c).wait()
    (forward_step if forward else backward_step)(step, slab_ref, wide_ref, sum_ref)

    @pl.when(step == D - 1)
    def _():
        if forward:
            rows = dot(jnp.concatenate(two_terms(sum_ref[...]), axis=0), reduce_ref[...])
            refs[-5][...] = pack_image((rows[:IMG] + rows[IMG:]) * scale_metric)
        else:
            sums = dot(sum_ref[...].reshape(D * VEC, WIDE).astype(BF), reduce_ref[...])
            rows = dot(fold_ref[...], jnp.concatenate(two_terms(sums), axis=1))
            parts = pack((rows[:, :128] + rows[:, 128:]) * scale_metric)
            first = core_ref[0] == 0
            refs[-6][...] = jnp.where(first, parts[0], parts[1])
            refs[-5][...] = jnp.where(first, parts[1], parts[0])


VECTOR = jax.ShapeDtypeStruct((PHYS, 32, 128), F32)
HALF = jax.ShapeDtypeStruct((32, 128), F32)


def sum_rows(count):
    return jax.ShapeDtypeStruct((count, 128), F32)


def apply_metric(forward, prologue, core, metric, constants, ins, outs):
    out_shape = list(outs) + ([HALF] if forward else [HALF, HALF])
    return pl.pallas_call(
        functools.partial(apply_kernel, forward, prologue, len(ins), len(outs)),
        grid=(D,),
        in_specs=[pl.BlockSpec(memory_space=pltpu.SMEM), pl.BlockSpec(memory_space=pl.ANY)]
        + [full(c.shape) for c in constants]
        + [full(i.shape) for i in ins],
        out_specs=[full(o.shape) for o in out_shape],
        out_shape=out_shape,
        scratch_shapes=[
            pltpu.VMEM((VEC if forward else IMG, WIDE), F32),
            pltpu.VMEM((IMG, WIDE) if forward else (D, VEC, WIDE), F32),
            pltpu.VMEM((D, SLAB, WIDE), BF),
            pltpu.SemaphoreType.DMA((D, SLAB // CHUNK)),
        ],
        compiler_params=pltpu.CompilerParams(vmem_limit_bytes=30 * 1024 * 1024),
        cost_estimate=pl.CostEstimate(flops=50_000_000, bytes_accessed=8_000_000, transcendentals=0),
        name="forward" if forward else "backward",
    )(core, pltpu.with_memory_space_constraint(metric, pltpu.HBM), *constants, *ins)


def first_vector(core_ref, ins, outs):
    return [ins[0][p] for p in range(PHYS)]


def share(a, b):
    return (shift_value / NCORE) * (a * b)


def sums_of(*groups):
    return jnp.concatenate([lane_sums(group) for group in groups], axis=0)


def first_image(core_ref, ins, outs):
    image = ins[0][...]
    start = [ins[1][p] for p in range(PHYS)]
    outs[0][...] = sums_of([image * image] + [share(v, v) for v in start], [v * v / NCORE for v in start])
    return image


def row(sums_ref, n):
    return jnp.sum(sums_ref[n : n + 1], axis=1, keepdims=True)


def next_residual(core_ref, ins, outs):
    own_ref, other_ref, start_ref, sums_ref = ins
    back = halves(core_ref, own_ref, other_ref)
    alpha = row(sums_ref, 1) / row(sums_ref, 0)
    residual = [start_ref[p] - alpha * (back[p] + shift_value * start_ref[p]) for p in range(PHYS)]
    for p in range(PHYS):
        outs[0][p] = residual[p]
    return residual


def next_image(core_ref, ins, outs):
    image, first = ins[0][...], ins[1][...]
    residual = [ins[2][p] for p in range(PHYS)]
    start = [ins[3][p] for p in range(PHYS)]
    outs[0][...] = sums_of(
        [image * image] + [share(r, r) for r in residual],
        [image * first] + [share(r, d) for r, d in zip(residual, start)],
        [r * r / NCORE for r in residual],
    )
    return image


def flatten(parts, expand_ref, own_ref):
    rest = unpack(parts)
    wide = None
    for _ in range(3):
        term = rest.astype(BF)
        rest = rest - term.astype(F32)
        piece = dot(term, expand_ref[...])
        wide = piece if wide is None else wide + piece
    own = own_ref[...].astype(F32)
    rows = [jnp.sum(wide[p * PAIR : (p + 1) * PAIR] * own, axis=0, keepdims=True) for p in range(PHYS)]
    return jnp.concatenate(rows, axis=0)[:, : DD * DD]


def finish_kernel(core_ref, expand_ref, own_lane_ref, half_0_ref, other_0_ref, half_1_ref, other_1_ref,
                  start_ref, residual_ref, sums_0_ref, sums_1_ref, solution_ref, out_ref):
    back_0 = halves(core_ref, half_0_ref, other_0_ref)
    back_r = halves(core_ref, half_1_ref, other_1_ref)
    curve_0, norm_0 = row(sums_0_ref, 0), row(sums_0_ref, 1)
    norm_1 = row(sums_1_ref, 2)
    alpha_0 = norm_0 / curve_0
    beta = norm_1 / norm_0
    curve_1 = row(sums_1_ref, 0) + beta * (2.0 * row(sums_1_ref, 1) + beta * curve_0)
    alpha_1 = norm_1 / curve_1
    answer, residual = [], []
    for p in range(PHYS):
        direction = residual_ref[p] + beta * start_ref[p]
        back = back_r[p] + beta * back_0[p] + shift_value * direction
        answer.append(alpha_0 * start_ref[p] + alpha_1 * direction)
        residual.append(residual_ref[p] - alpha_1 * back)
    solution_ref[0] = flatten(answer, expand_ref, own_lane_ref)
    out_ref[0] = flatten(residual, expand_ref, own_lane_ref)


def finish(core, *ins):
    field = jax.ShapeDtypeStruct((1, PHYS, DD * DD), F32)
    return pl.pallas_call(
        finish_kernel,
        in_specs=[pl.BlockSpec(memory_space=pltpu.SMEM)] + [full(i.shape) for i in ins],
        out_specs=[full(field.shape)] * 2,
        out_shape=[field, field],
        compiler_params=pltpu.CompilerParams(vmem_limit_bytes=16 * 1024 * 1024),
        name="finish",
    )(core, *ins)


def spread(value, axes, count):
    return lax.all_to_all(jnp.broadcast_to(value[None], (count,) + value.shape), axes, 0, 0, tiled=True)


def swap(value):
    return lax.ppermute(value, "core", [(0, 1), (1, 0)])


def sum_sites(lanes):
    for step in (1, 2):
        lanes = lanes + lax.ppermute(lanes, "site", [(i, i ^ step) for i in range(NSITE)])
    return lanes


def sum_chips(value, lanes=None, cores=False):
    parts = spread(value.astype(BF), ("x", "z"), CHIPS)
    if lanes is not None:
        lanes = sum_sites(lanes)
        if cores:
            lanes = lanes + swap(lanes)
        parts, lanes = lax.optimization_barrier((parts, lanes))
    return jnp.sum(parts.astype(F32), axis=0), lanes


def sum_halves(keep, send, lanes):
    half, lanes = sum_chips(keep + swap(send), lanes, True)
    return half, swap(half), lanes


def to_packed(field):
    move = np.zeros((2, 32, DD), np.float32)
    for dk in range(D):
        for rk in range(D):
            move[rk // 4, rk % 4 * GROUP + dk, dk * D + rk] = 1
    grid = jnp.einsum("hrc,pkc->prhk", move, field.reshape(PHYS, DD, DD), precision=lax.Precision.HIGHEST)
    return jnp.pad(grid, ((0, 0), (0, 0), (0, 0), (0, 64 - DD))).reshape(PHYS, 32, 128)


def ring(value, step):
    return lax.ppermute(value, "z", [(i, (i + step) % NZ) for i in range(NZ)])


def body(upper, corner_low, edge_bottom, corner_right, edge_right, right_side):
    core = lax.axis_index("core")

    mixed = jnp.einsum("ih,hgq->giq", corner_low[0], edge_bottom[0], preferred_element_type=F32).astype(BF)
    mixed = mixed.reshape(4, 64, 4, DD).transpose(1, 0, 2, 3)

    cols = jnp.einsum("efr,gf->reg", edge_right[0], corner_right[0], preferred_element_type=F32).astype(BF)
    cols = jnp.pad(cols.reshape(D, D, 4, CHI), ((0, 0), (0, 1), (0, 0), (0, 0))).reshape(D, NCORE, RB, 4, CHI)
    mine = lax.dynamic_index_in_dim(cols, core, 1, keepdims=False)
    other = swap(lax.dynamic_index_in_dim(cols, 1 - core, 1, keepdims=False))
    cols = jnp.stack([jnp.where(core == 0, mine, other), jnp.where(core == 0, other, mine)], axis=2)
    cols = spread(cols.reshape(D * RB * 8 * CHI // 128, 128), "x", NX)
    cols = cols.reshape(NX, D * RB, 8, CHI).transpose(1, 0, 2, 3).reshape(D * RB, 8 * NX, CHI)

    row = jnp.arange(CHI)
    z = (lax.axis_index("z") + jnp.asarray(OFFSETS)[row // 32] + NZ) % NZ
    place = (row // 8 % NX * NZ + z) * 8 + row % 8
    pick = (place[:, None] == jnp.arange(CHI)[None, :]).astype(BF)
    own = jnp.einsum("je,iek->ikj", pick, upper[0], preferred_element_type=F32).astype(BF)
    own = jnp.pad(own, ((0, 0), (0, WIDE - DD * DD), (0, 0)))

    cols, mixed, own = lax.optimization_barrier((cols, mixed, own))
    other = swap(own)
    up, down = [cols], [cols]
    for _ in range(2):
        up.append(ring(up[-1], 1))
        down.append(ring(down[-1], -1))

    rows = np.zeros((PAIR, DD), np.float32)
    rows[np.arange(DD) // D * GROUP + np.arange(DD) % D, np.arange(DD)] = 1
    mixed = lax.all_to_all(mixed, ("x", "z", "core"), 0, 0, tiled=True).reshape(CHI, 4, DD)
    mixed = jnp.einsum("rq,giq->irg", jnp.asarray(rows, BF), mixed, preferred_element_type=F32).astype(BF)
    mixed = mixed.reshape(4 * PAIR, CHI)
    mixed = jnp.concatenate([mixed, swap(mixed)], axis=0)
    start = to_packed(right_side[0])

    up.append(ring(up[-1], 1))
    down.append(ring(down[-1], -1))
    metric = build_metric(mixed, [cols, up[1], down[1], up[2]], own, other)
    far_up, far_down, metric = lax.optimization_barrier((up[3], down[3], metric))
    last = [ring(far_up[: D * RB // 2], 1), ring(far_down[D * RB // 2 :], -1)]
    metric = build_metric(mixed, [down[2], far_up, far_down, *last], own, other, metric)

    first, second, fold, own_lane = (jnp.asarray(t, BF) for t in tables())
    flag = core.astype(jnp.int32).reshape(1)
    forward = functools.partial(apply_metric, True)
    backward = functools.partial(apply_metric, False)
    ahead, behind = (first, second.T, fold), (second, first.T, fold)

    (part,) = forward(first_vector, flag, metric, ahead, [start], [])
    image, _ = sum_chips(part)
    sums_0, keep, send = backward(first_image, flag, metric, behind, [image, start], [sum_rows(2)])
    half_0, other_0, sums_0 = sum_halves(keep, send, sums_0)
    residual, part = forward(next_residual, flag, metric, ahead, [half_0, other_0, start, sums_0], [VECTOR])
    image_r, _ = sum_chips(part)
    sums_1, keep, send = backward(next_image, flag, metric, behind, [image_r, image, residual, start], [sum_rows(3)])
    half_1, other_1, sums_1 = sum_halves(keep, send, sums_1)
    return finish(flag, first, own_lane, half_0, other_0, half_1, other_1, start, residual, sums_0, sums_1)


def solution(mesh):
    split = Mesh(mesh.devices.reshape(NX, NZ, NCORE, NSITE), ("x", "z", "core", "site"))
    chi = ("x", "z", "core")
    placed = (
        P("site", chi, None, None),
        P("site", None, None),
        P("site", None, chi, None),
        P("site", None, None),
        P("site", chi, None, None),
        P("site", None, None),
    )
    return jax.shard_map(
        body,
        mesh=split,
        in_specs=placed,
        out_specs=(P("site", None, None), P("site", None, None)),
        check_vma=False,
    )
```
